256 devices in a mesh: pts: 128 (over z, x, y), rep: 2 (over core).
Axes of the slice: x: 4, y: 4, z: 8, core: 2. Of those that a mesh axis runs over, the one named last changes fastest.
Arguments:
- points: bfloat16 [262144, 256], P(('rep', 'pts')), parts along dimension 0, may hold values from -6 to 6
- order: int32 [2, 262144], P(None, ('rep', 'pts')), parts along dimension 1, may hold values from 0 to 131071, as said below
- norm_gains: float32 [2, 2, 256], replicated, may hold values from 0.25 to 1.75
- qkv_weight: bfloat16 [2, 256, 768], replicated, may hold values from -4 to 4
- proj_weight: bfloat16 [2, 256, 256], replicated, may hold values from -0.375 to 0.375
- up_weight: bfloat16 [2, 256, 1024], replicated, may hold values from -0.375 to 0.375
- down_weight: bfloat16 [2, 1024, 256], replicated, may hold values from -0.1875 to 0.1875
Outputs:
- encoded: bfloat16 [262144, 256], P(('rep', 'pts')), parts along dimension 0
The draws below stay inside these ranges and needn't reach their ends.
There are 2 independent parts, one for each index of `rep`. The reference program is written for one: setup_inputs(seed, part) draws one part's arguments, and reference() takes and returns one part's arrays. A program takes and returns all parts, laid end to end along the dimension named above; an argument that names none is the same for every part. Nothing has to cross between parts.
Inputs may be any that keep to these rules, and one draw needn't show every extreme that they name: For each block, order[b] is a permutation of 0 to 131071. Split serial positions into devices of 1024 positions and those into patches of 1024; for each block, at most 16 of the 1024 points of one device go into one patch of one device, and in every block some device sends exactly 16 points into some patch.
All inputs are finite; a program needn't handle non-finite values.
Results may differ from the reference program's by a relative error of at most 0.035.
The reference program's roundings to bfloat16 on the way count: a program that leaves them out, or rounds other values in their place, can miss the bound.
Values may be sent and summed in bfloat16 or wider, within the bound.
A program may use at most 64 MiB of HBM per device.

```python
import jax
import jax.numpy as jnp
from jax import lax

WIDTH = 256
MLP_WIDTH = 1024
HEADS = 16
PATCH = 1024
BLOCKS = 2
ROWS_DEV = 1024
POINTS = 131072
N_PTS = 128


def circulant_half(rng_key, groups, most):
    upper = jax.random.randint(rng_key, (groups // 2,), 0, most + 1)
    upper = upper.at[0].set(most)
    return jnp.concatenate([upper, most - upper])


def pair_counts(rng_key, groups, most):
    key_first, key_second, key_shift, key_other = jax.random.split(rng_key, 4)
    first = circulant_half(key_first, groups, most)
    second = circulant_half(key_second, groups, most)
    shift_one = jax.random.randint(key_shift, (), 0, groups)
    shift_two = (2 * jax.random.randint(key_other, (), 0, groups // 2) + shift_one) % groups
    source = jnp.arange(groups)[:, None]
    target = jnp.arange(groups)[None, :]
    return first[(target - source + shift_one) % groups] + second[(target + source + shift_two) % groups]


def block_order(rng_key, groups, per_dev, patch, rows_dev):
    most = patch // groups
    counts = jnp.stack([pair_counts(jax.random.fold_in(rng_key, 100 + index), groups, most) for index in range(per_dev)], axis=2)
    flat_counts = counts.reshape(groups, groups * per_dev)

    def source_labels(count_row):
        return jnp.repeat(jnp.arange(groups * per_dev), count_row, total_repeat_length=rows_dev)
    labels = jax.vmap(source_labels)(flat_counts)
    starts = jnp.cumsum(flat_counts, axis=1) - flat_counts
    ranks = jnp.arange(rows_dev)[None, :] - jnp.take_along_axis(starts, labels, axis=1)
    before = jnp.cumsum(flat_counts, axis=0) - flat_counts
    offsets = jnp.take_along_axis(before, labels, axis=1) + ranks
    slot_keys = jax.random.split(jax.random.fold_in(rng_key, 7), groups * per_dev)
    slot_perm = jax.vmap(lambda sub_key: jax.random.permutation(sub_key, patch))(slot_keys)
    slots = slot_perm[labels, offsets]
    targets = labels // per_dev
    patch_index = labels % per_dev
    positions = targets * rows_dev + patch_index * patch + slots
    row_keys = jax.random.split(jax.random.fold_in(rng_key, 9), groups)
    row_perm = jax.vmap(lambda sub_key: jax.random.permutation(sub_key, rows_dev))(row_keys)
    placed = jnp.zeros((groups, rows_dev), jnp.int32).at[jnp.arange(groups)[:, None], row_perm].set(positions.astype(jnp.int32))
    return placed.reshape(groups * rows_dev)


def draw_order(key, part):
    key = jax.random.fold_in(key, 11)
    return jnp.stack([block_order(jax.random.fold_in(key, index), N_PTS, ROWS_DEV // PATCH, PATCH, ROWS_DEV) for index in range(BLOCKS)]).astype(jnp.int32)


def draw_qkv_weight(key, part):
    key = jax.random.fold_in(key, 5)
    base_draw = jax.random.normal(key, (BLOCKS, WIDTH, 3 * WIDTH), jnp.float32) * WIDTH ** (-0.5)
    return base_draw.astype(jnp.bfloat16)


def shard_levels(own_key, extent, shards, least, top_value):
    loudness = 1.0
    for axis_at, parts in shards:
        steps = jax.random.uniform(jax.random.fold_in(jax.random.fold_in(own_key, 6), axis_at), (parts,), jnp.float32, least / len(shards), top_value / len(shards))
        loudness = loudness * jnp.repeat(jnp.exp(steps), extent[axis_at] // parts).reshape((-1,) + (1,) * (len(extent) - 1 - axis_at))
    return loudness


def gaussian(rng, shape, spread, reach, pieces=(), dtype=jnp.bfloat16):
    values = jax.random.normal(rng, shape, jnp.float32) * spread
    if len(pieces) > 0:
        values = shard_levels(rng, shape, pieces, -0.22, 0.18) * values
    return jnp.clip(values, min=-reach, max=reach).astype(dtype)


def setup_inputs(seed: int = 0, part: int = 0) -> dict:
    arg_keys = jax.random.split(jax.random.key(seed), 8)
    part_splits = jax.random.split(jax.random.fold_in(arg_keys[7], part), 8)
    return {
        "points": gaussian(part_splits[0], (POINTS, WIDTH), 1.0, 6.0, ((0, 128),)),
        "order": draw_order(jax.random.fold_in(jax.random.fold_in(arg_keys[7], part), 71), part),
        "norm_gains": jnp.clip(1.0 + 0.15 * jax.random.normal(arg_keys[2], (BLOCKS, 2, WIDTH), jnp.float32), 0.25, 1.75),
        "qkv_weight": draw_qkv_weight(jax.random.fold_in(arg_keys[7], 71), part),
        "proj_weight": gaussian(arg_keys[4], (BLOCKS, WIDTH, WIDTH), WIDTH ** -0.5, 0.375),
        "up_weight": gaussian(arg_keys[5], (BLOCKS, WIDTH, MLP_WIDTH), WIDTH ** -0.5, 0.375),
        "down_weight": gaussian(arg_keys[6], (BLOCKS, MLP_WIDTH, WIDTH), MLP_WIDTH ** -0.5, 0.1875),
    }


EPS = 1e-05

def layer_norm(features, gain):
    features = features.astype(jnp.float32)
    average = lax.optimization_barrier(jnp.mean(features, axis=-1, keepdims=True))
    centered = features - average
    variance = lax.optimization_barrier(jnp.mean(centered * centered, axis=-1, keepdims=True))
    return centered * lax.rsqrt(variance + EPS) * gain

def patch_attention(projected, heads):
    length = projected.shape[0]
    channels = projected.shape[1] // 3
    head_size = channels // heads
    split_rows = jnp.transpose(projected.reshape(length, 3, heads, head_size), (1, 2, 0, 3))
    score_scale = head_size ** (-0.5)

    def one_head(operands):
        queries, keys, values = operands
        scores = jnp.dot(queries, keys.T, preferred_element_type=jnp.float32) * score_scale
        row_peak = lax.optimization_barrier(jnp.max(scores, axis=1, keepdims=True))
        weights = jnp.exp(scores - row_peak)
        weights = (weights / lax.optimization_barrier(jnp.sum(weights, axis=1, keepdims=True))).astype(jnp.bfloat16)
        return jnp.dot(weights, values, preferred_element_type=jnp.float32).astype(jnp.bfloat16)
    attended = lax.map(one_head, (split_rows[0], split_rows[1], split_rows[2]))
    return jnp.transpose(attended, (1, 0, 2)).reshape(length, channels)

def mixer(serial_rows, gain_first, qkv_matrix, proj_matrix):
    normed = layer_norm(serial_rows, gain_first).astype(jnp.bfloat16)
    projected = jnp.dot(normed, qkv_matrix, preferred_element_type=jnp.float32).astype(jnp.bfloat16)
    attended = patch_attention(projected, HEADS)
    branch = jnp.dot(attended, proj_matrix, preferred_element_type=jnp.float32)
    return (serial_rows.astype(jnp.float32) + branch).astype(jnp.bfloat16)

def feed(middle, gain_second, up_matrix, down_matrix):
    second = layer_norm(middle, gain_second).astype(jnp.bfloat16)
    lifted = jax.nn.gelu(jnp.dot(second, up_matrix, preferred_element_type=jnp.float32), approximate=False).astype(jnp.bfloat16)
    branch = jnp.dot(lifted, down_matrix, preferred_element_type=jnp.float32)
    return (middle.astype(jnp.float32) + branch).astype(jnp.bfloat16)

def reference(points, order, norm_gains, qkv_weight, proj_weight, up_weight, down_weight):
    current = points
    for layer_index in range(BLOCKS):
        positions = order[layer_index]
        serial = jnp.zeros_like(current).at[positions].set(current)
        patches = serial.reshape(POINTS // PATCH, PATCH, WIDTH)

        def run_patch(patch_rows):
            middle = mixer(patch_rows, norm_gains[layer_index, 0], qkv_weight[layer_index], proj_weight[layer_index])
            return feed(middle, norm_gains[layer_index, 1], up_weight[layer_index], down_weight[layer_index])
        output = lax.map(run_patch, patches).reshape(POINTS, WIDTH)
        current = output[positions]
    return current
```

```python
import functools

import jax
import jax.numpy as jnp
from jax import lax
from jax.experimental import pallas as pl
from jax.experimental.pallas import tpu as pltpu
from jax.sharding import PartitionSpec as P

HEADS = 16
PATCH = 1024
BLOCKS = 2
WIDTH = 256
MLP = 1024
N = 128
CAP = 16
HALF = 512
EPS = 1e-05

F32 = jnp.float32
BF16 = jnp.bfloat16
I32 = jnp.int32
MESH = pl.DeviceIdType.MESH


def iota(shape, dim):
    return lax.broadcasted_iota(I32, shape, dim)


def one_hot(mask):
    return jnp.where(mask, 1.0, 0.0).astype(BF16)


def mm(a, b):
    return jnp.dot(a, b, preferred_element_type=F32)


def mm_nt(a, b):
    return lax.dot_general(a, b, (((1,), (1,)), ((), ())), preferred_element_type=F32)


def layer_norm(features, gain):
    features = features.astype(F32)
    average = jnp.mean(features, axis=-1, keepdims=True)
    centered = features - average
    variance = jnp.mean(centered * centered, axis=-1, keepdims=True)
    return (centered * lax.rsqrt(variance + EPS) * gain).astype(BF16)


def soften(s_ref, w_ref):
    for r in range(0, HALF, 16):
        s = s_ref[r : r + 16, :]
        p = jnp.exp(s - jnp.max(s, axis=1, keepdims=True))
        w_ref[r : r + 16, :] = (p * (1.0 / jnp.sum(p, axis=1, keepdims=True))).astype(BF16)


def attend(row0, q_ref, kt_ref, v_ref, acc_ref, s0, s1, w0, w1):
    lane = iota((1, WIDTH), 1) // (WIDTH // HEADS)

    def score(h, s_ref):
        q = q_ref[pl.ds(row0, HALF), :]
        s_ref[...] = mm(jnp.where(lane == h, q, 0).astype(BF16), kt_ref[...])

    def mix(h, w_ref):
        o = mm(w_ref[...], v_ref[...])
        acc_ref[...] = jnp.where(lane == h, o, acc_ref[...])

    score(0, s0)
    score(1, s1)
    soften(s0, w0)

    def body(j, carry):
        h = 2 * j + 1
        score(h + 1, s0)
        soften(s1, w1)
        mix(h - 1, w0)
        score(h + 2, s1)
        soften(s0, w0)
        mix(h, w1)
        return carry

    lax.fori_loop(0, HEADS // 2 - 1, body, 0)
    soften(s1, w1)
    mix(HEADS - 2, w0)
    mix(HEADS - 1, w1)


def kernel(
    points, order, gains, wqkv, wproj, wup, wdown,
    out,
    current, send, fwd, ret_send, ret, counts_send, counts,
    compact, serial, q, kt, v, acc, s0, s1, w0, w1, finished,
    fwd_ss, fwd_rs, ret_ss, ret_rs, cnt_ss, cnt_rs,
):
    me = lax.axis_index("pts")
    barrier = pltpu.get_barrier_semaphore()

    @pl.loop(1, N)
    def _(i):
        pl.semaphore_signal(
            barrier, inc=1, device_id={"pts": lax.rem(me + i, N)}, device_id_type=MESH
        )

    def remote(src, dst, ss, rs, t):
        return pltpu.make_async_remote_copy(
            src_ref=src, dst_ref=dst, send_sem=ss, recv_sem=rs,
            device_id={"pts": t}, device_id_type=MESH,
        )

    def all_of(buf, ss, rs):
        part = buf.at[pl.ds(0, N - 1)]
        return remote(part, part, ss, rs, lax.rem(me + 1, N))

    def plan(b):
        target = order[pl.ds(b, 1), :] // PATCH
        to = one_hot(iota((N, PATCH), 0) == target)
        before = one_hot(iota((PATCH, PATCH), 0) < iota((PATCH, PATCH), 1))
        rank = jnp.sum(to.astype(F32) * mm(to, before), axis=0, keepdims=True).astype(I32)
        count = mm_nt(jnp.ones((8, PATCH), BF16), to)
        return target, rank, count

    target0, rank0, count0 = plan(0)
    target1, rank1, count1 = plan(1)
    counts_send[...] = count0 + 32.0 * count1
    targets = (target0, target1)
    ranks = (rank0, rank1)

    pl.semaphore_wait(barrier, N - 1)

    @pl.loop(1, N)
    def _(i):
        t = lax.rem(me + i, N)
        remote(
            counts_send.at[pl.ds(0, 1), :], counts.at[me, pl.ds(0, 1), :], cnt_ss, cnt_rs, t
        ).start()

    counts[me] = counts_send[...]

    my_y = lax.rem(me, 4)

    def forward(b, rows_ref):
        target, rank = targets[b], ranks[b]
        slot = (target // 4) * CAP + rank
        for i in range(4):
            y = lax.rem(my_y + i, 4)
            mine = jnp.where(lax.rem(target, 4) == y, slot, -1)
            pick = one_hot(iota((32 * CAP, PATCH), 0) == mine)
            rows = mm(pick, rows_ref[...]).astype(BF16).reshape(32, CAP, WIDTH)
            send[pl.ds(y * 32, 32)] = rows

            @pl.loop(0, 32)
            def _(j):
                tj = lax.rem(me // 4 + j, 32)
                t = tj * 4 + y

                @pl.when(t != me)
                def _():
                    remote(
                        send.at[y * 32 + tj], fwd.at[b, me], fwd_ss.at[b], fwd_rs.at[b], t
                    ).start()

        fwd[b, me] = send[my_y * 32 + me // 4]

    forward(0, points)

    d = remote(
        counts.at[pl.ds(0, N - 1), pl.ds(0, 1), :], counts.at[pl.ds(0, N - 1), pl.ds(0, 1), :],
        cnt_ss, cnt_rs, lax.rem(me + 1, N),
    )
    d.wait_send()
    d.wait_recv()
    table = counts[:, 0, :].astype(I32)

    def places(b):
        count = (table % 32) if b == 0 else (table // 32)
        mine = one_hot(iota((N, N), 0) == me)
        n = mm(count.astype(F32).astype(BF16), mine)
        lane = iota((N, N), 1)
        slot = lane % CAP
        valid = n > slot.astype(F32)
        used = one_hot(valid)
        above = one_hot(iota((N, N), 0) > iota((N, N), 1))
        earlier = mm(above, used)
        total = mm(jnp.ones((N, N), BF16), used).astype(BF16)
        higher = one_hot((iota((N, N), 0) > slot) & (iota((N, N), 0) < CAP))
        place = jnp.where(valid, (earlier + mm(total, higher)).astype(I32), -1)
        coded = jnp.where(lane < CAP, place >> 4, jnp.where(lane < 2 * CAP, place & 15, 0))
        return coded.astype(F32)

    def fill_compact(coded):
        coded_t = coded.T.astype(BF16)
        spread = one_hot(iota((N, N * CAP), 0) == iota((N, N * CAP), 1) // CAP)
        x = mm(coded_t[0 : 2 * CAP, :], spread)
        row = iota((2 * CAP, N * CAP), 0)
        k = iota((2 * CAP, N * CAP), 1) % CAP
        x = jnp.where(row == k, 16.0 * x, jnp.where(row == k + CAP, x, 0.0))
        place = jnp.sum(x, axis=0, keepdims=True).astype(I32)
        for r in range(0, PATCH, 256):
            compact[r : r + 256, :] = one_hot(iota((256, N * CAP), 0) + r == place)

    def half_places(coded, half):
        spread = one_hot(iota((N * 8, N), 1) == iota((N * 8, N), 0) // 8)
        x = mm(spread, coded.astype(BF16))
        lane = iota((N * 8, N), 1)
        k = iota((N * 8, N), 0) % 8 + (8 if half == 0 else 0)
        x = jnp.where(lane == k, 16.0 * x, jnp.where(lane == k + CAP, x, 0.0))
        return jnp.sum(x, axis=1, keepdims=True).astype(I32)

    def columns(b):
        target = jnp.broadcast_to(targets[b].astype(F32), (N, PATCH)).T.astype(I32)
        rank = jnp.broadcast_to(ranks[b].astype(F32), (N, PATCH)).T.astype(I32)
        return target[:, 0:1], rank[:, 0:1]

    for b in range(BLOCKS):
        coded = places(b)
        fill_compact(coded)
        target_col, rank_col = columns(b)

        d = all_of(fwd.at[b], fwd_ss.at[b], fwd_rs.at[b])
        d.wait_send()
        d.wait_recv()
        for r in range(0, PATCH, 256):
            rows = mm(compact[r : r + 256, :], fwd[b].reshape(N * CAP, WIDTH)).astype(BF16)
            serial[r : r + 256, :] = rows
            normed = layer_norm(rows, gains[b, 0:1, :])
            projected = mm(normed, wqkv[b]).astype(BF16)
            q[r : r + 256, :] = projected[:, 0:WIDTH] * jnp.asarray(0.25, BF16)
            kt[:, r : r + 256] = projected[:, WIDTH : 2 * WIDTH].astype(F32).T.astype(BF16)
            v[r : r + 256, :] = projected[:, 2 * WIDTH :]

        for half in range(2):
            attend(half * HALF, q, kt, v, acc, s0, s1, w0, w1)
            for r in range(0, HALF, 256):
                g = half * HALF + r
                branch = mm(acc[r : r + 256, :].astype(BF16), wproj[b])
                middle = (serial[g : g + 256, :].astype(F32) + branch).astype(BF16)
                second = layer_norm(middle, gains[b, 1:2, :])
                up = mm(second, wup[b])
                lifted = (up * (1.0 + lax.erf(up * (0.5**0.5))) * 0.5).astype(BF16)
                finished[g : g + 256, :] = (
                    middle.astype(F32) + mm(lifted, wdown[b])
                ).astype(BF16)
            known = HALF * (half + 1)
            pick = one_hot(iota((N * 8, known), 1) == half_places(coded, half))
            if b > 0:
                all_of(ret_send.at[half], ret_ss.at[b - 1, half], ret_rs.at[b - 1, half]).wait_send()
            ret_send[half] = mm(pick, finished[0:known, :]).astype(BF16).reshape(N, 8, WIDTH)

            @pl.loop(1, N)
            def _(i):
                t = lax.rem(me + i, N)
                remote(
                    ret_send.at[half, t], ret.at[b, half, me],
                    ret_ss.at[b, half], ret_rs.at[b, half], t,
                ).start()

            ret[b, half, me] = ret_send[half, me]

        total = None
        for half in range(2):
            all_of(ret.at[b, half], ret_ss.at[b, half], ret_rs.at[b, half]).wait_recv()
            slot = target_col * 8 + rank_col - (8 if half == 0 else 0)
            here = (rank_col >= 8) if half == 0 else (rank_col < 8)
            slot = jnp.where(here, slot, -1)
            pick = one_hot(iota((PATCH, N * 8), 1) == slot)
            part = mm(pick, ret[b, half].reshape(N * 8, WIDTH))
            total = part if total is None else total + part
        if b + 1 < BLOCKS:
            current[...] = total.astype(BF16)
            forward(b + 1, current)
        else:
            out[...] = total.astype(BF16)

    for half in range(2):
        all_of(
            ret_send.at[half], ret_ss.at[BLOCKS - 1, half], ret_rs.at[BLOCKS - 1, half]
        ).wait_send()


def per_device(points, order, norm_gains, qkv_weight, proj_weight, up_weight, down_weight):
    vm = pl.BlockSpec(memory_space=pltpu.VMEM)
    dma = pltpu.SemaphoreType.DMA
    return pl.pallas_call(
        kernel,
        out_shape=jax.ShapeDtypeStruct((PATCH, WIDTH), BF16),
        in_specs=[vm] * 7,
        out_specs=vm,
        scratch_shapes=[
            pltpu.VMEM((PATCH, WIDTH), BF16),
            pltpu.VMEM((N, CAP, WIDTH), BF16),
            pltpu.VMEM((BLOCKS, N, CAP, WIDTH), BF16),
            pltpu.VMEM((2, N, 8, WIDTH), BF16),
            pltpu.VMEM((BLOCKS, 2, N, 8, WIDTH), BF16),
            pltpu.VMEM((8, N), F32),
            pltpu.VMEM((N, 8, N), F32),
            pltpu.VMEM((PATCH, N * CAP), BF16),
            pltpu.VMEM((PATCH, WIDTH), BF16),
            pltpu.VMEM((PATCH, WIDTH), BF16),
            pltpu.VMEM((WIDTH, PATCH), BF16),
            pltpu.VMEM((PATCH, WIDTH), BF16),
            pltpu.VMEM((HALF, WIDTH), F32),
            pltpu.VMEM((HALF, PATCH), F32),
            pltpu.VMEM((HALF, PATCH), F32),
            pltpu.VMEM((HALF, PATCH), BF16),
            pltpu.VMEM((HALF, PATCH), BF16),
            pltpu.VMEM((PATCH, WIDTH), BF16),
            dma((BLOCKS,)), dma((BLOCKS,)),
            dma((BLOCKS, 2)), dma((BLOCKS, 2)),
            dma, dma,
        ],
        compiler_params=pltpu.CompilerParams(
            collective_id=0, has_side_effects=True, vmem_limit_bytes=56 * 2**20
        ),
        name="encoder",
    )(points, order, norm_gains, qkv_weight, proj_weight, up_weight, down_weight)


def solution(mesh):
    in_specs = (P(("rep", "pts"), None), P(None, ("rep", "pts")), P(), P(), P(), P(), P())
    out_specs = P(("rep", "pts"), None)
    return jax.shard_map(
        per_device, mesh=mesh, in_specs=in_specs, out_specs=out_specs, check_vma=False
    )
```

```python
import functools

import jax
import jax.numpy as jnp
from jax import lax
from jax.experimental import pallas as pl
from jax.experimental.pallas import tpu as pltpu
from jax.sharding import PartitionSpec as P

HEADS = 16
PATCH = 1024
BLOCKS = 2
WIDTH = 256
MLP = 1024
N = 128
CAP = 16
CHUNK = 256
EPS = 1e-05

F32 = jnp.float32
BF16 = jnp.bfloat16
I32 = jnp.int32
MESH = pl.DeviceIdType.MESH


def iota(shape, dim):
    return lax.broadcasted_iota(I32, shape, dim)


def one_hot(mask):
    return jnp.where(mask, 1.0, 0.0).astype(BF16)


def mm(a, b):
    return jnp.dot(a, b, preferred_element_type=F32)


def mm_nt(a, b):
    return lax.dot_general(a, b, (((1,), (1,)), ((), ())), preferred_element_type=F32)


def layer_norm(features, gain):
    features = features.astype(F32)
    average = jnp.mean(features, axis=-1, keepdims=True)
    centered = features - average
    variance = jnp.mean(centered * centered, axis=-1, keepdims=True)
    return (centered * lax.rsqrt(variance + EPS) * gain).astype(BF16)


def soften(s_ref, w_ref):
    for r in range(0, CHUNK, 16):
        s = s_ref[r : r + 16, :]
        p = jnp.exp(s - jnp.max(s, axis=1, keepdims=True))
        w_ref[r : r + 16, :] = (p * (1.0 / jnp.sum(p, axis=1, keepdims=True))).astype(BF16)


def repeat(low, high, width, body):
    steps = (high - low) // width

    @pl.loop(0, steps)
    def _(j):
        for u in range(width):
            body(low + j * width + u)

    for i in range(low + steps * width, high):
        body(i)


def kernel(
    points, order, gains, wqkv_hbm, wproj_hbm, wup_hbm, wdown_hbm,
    out,
    wqkv, wproj, wup, wdown,
    current, send, fwd, ret_send, ret, counts_send, counts,
    compact, g_pick, r_pick, e_pick,
    gathered, serial, q, kt, v, acc, s0, s1, w0, w1, finished,
    fwd_ss, fwd_rs, ret_ss, ret_rs, cnt_ss, cnt_rs, load_sem,
):
    me = lax.axis_index("pts")
    my_y = lax.rem(me, 4)
    my_j = me // 4
    barrier = pltpu.get_barrier_semaphore()

    repeat(
        1, N, 6,
        lambda i: pl.semaphore_signal(
            barrier, inc=1, device_id={"pts": lax.rem(me + i, N)}, device_id_type=MESH
        ),
    )
    loads = [
        pltpu.make_async_copy(a, b, load_sem.at[i])
        for i, (a, b) in enumerate(
            ((wqkv_hbm, wqkv), (wproj_hbm, wproj), (wup_hbm, wup), (wdown_hbm, wdown))
        )
    ]
    for load in loads:
        load.start()

    def remote(src, dst, ss, rs, t):
        return pltpu.make_async_remote_copy(
            src_ref=src, dst_ref=dst, send_sem=ss, recv_sem=rs,
            device_id={"pts": t}, device_id_type=MESH,
        )

    def many(part, ss, rs):
        return remote(part, part, ss, rs, lax.rem(me + 1, N))

    def plan(b):
        target = order[pl.ds(b, 1), :] // PATCH
        to = one_hot(iota((N, PATCH), 0) == target)
        before = one_hot(iota((PATCH, PATCH), 0) < iota((PATCH, PATCH), 1))
        rank = jnp.sum(to.astype(F32) * mm(to, before), axis=0, keepdims=True).astype(I32)
        count = mm_nt(jnp.ones((8, PATCH), BF16), to)
        return target, rank, count

    plans = [plan(b) for b in range(BLOCKS)]
    counts_send[...] = plans[0][2] + 32.0 * plans[1][2]

    def fill_g(b):
        target, rank, _ = plans[b]
        slot = (target // 4) * CAP + rank
        for y in range(4):
            mine = jnp.where(lax.rem(target, 4) == y, slot, -1)
            g_pick[y] = one_hot(iota((32 * CAP, PATCH), 0) == mine)

    def fill_r(b):
        target = jnp.broadcast_to(plans[b][0].astype(F32), (N, PATCH)).T.astype(I32)[:, 0:1]
        rank = jnp.broadcast_to(plans[b][1].astype(F32), (N, PATCH)).T.astype(I32)[:, 0:1]
        place = (target % 64) * 8 + (target // 64) * 4
        for c in range(4):
            low = 12 - 4 * c
            here = (rank >= low) & (rank < low + 4)
            slot = jnp.where(here, place + rank - low, -1)
            r_pick[c] = one_hot(iota((PATCH, 512), 1) == slot)

    def stage(i, rows_ref):
        y = lax.rem(my_y + i, 4)
        rows = mm(g_pick[y], rows_ref[...]).astype(BF16).reshape(32, CAP, WIDTH)
        send[pl.ds(y * 32, 32)] = rows

    def launch(b, i):
        y = lax.rem(my_y + i, 4)

        def one(j):
            tj = lax.rem(my_j + j, 32)
            remote(
                send.at[y * 32 + tj], fwd.at[b, my_y * 32 + my_j],
                fwd_ss.at[b], fwd_rs.at[b, i], tj * 4 + y,
            ).start()

        if i == 0:
            fwd[b, my_y * 32 + my_j] = send[my_y * 32 + my_j]
            repeat(1, 32, 8, one)
        else:
            repeat(0, 32, 8, one)

    fill_g(0)
    for i in range(4):
        stage(i, points)

    pl.semaphore_wait(barrier, N - 1)

    repeat(
        1, N, 6,
        lambda i: remote(
            counts_send.at[pl.ds(0, 1), :], counts.at[me, pl.ds(0, 1), :], cnt_ss, cnt_rs,
            lax.rem(me + i, N),
        ).start(),
    )
    counts[me] = counts_send[...]
    for i in range(4):
        launch(0, i)

    fill_g(1)
    fill_r(0)

    d = many(counts.at[pl.ds(0, N - 1), pl.ds(0, 1), :], cnt_ss, cnt_rs)
    d.wait_send()
    d.wait_recv()
    table = counts[:, 0, :].astype(I32)

    def places(b):
        count = (table % 32) if b == 0 else (table // 32)
        mine = one_hot(iota((N, N), 0) == me)
        n = mm(count.astype(F32).astype(BF16), mine)
        lane = iota((N, N), 1)
        slot = lane % CAP
        valid = n > slot.astype(F32)
        used = one_hot(valid)
        above = one_hot(iota((N, N), 0) > iota((N, N), 1))
        earlier = mm(above, used)
        total = mm(jnp.ones((N, N), BF16), used).astype(BF16)
        higher = one_hot((iota((N, N), 0) > slot) & (iota((N, N), 0) < CAP))
        place = jnp.where(valid, (earlier + mm(total, higher)).astype(I32), -1)
        coded = jnp.where(lane < CAP, place >> 4, jnp.where(lane < 2 * CAP, place & 15, 0))
        return coded.astype(F32)

    def fill_compact(coded):
        coded_t = coded.T.astype(BF16)[0 : 2 * CAP, :]
        row = iota((2 * CAP, 512), 0)
        k = iota((2 * CAP, 512), 1) % CAP
        for y in range(4):
            x = mm(coded_t, one_hot(iota((N, 512), 0) == iota((N, 512), 1) // CAP * 4 + y))
            x = jnp.where(row == k, 16.0 * x, jnp.where(row == k + CAP, x, 0.0))
            place = jnp.sum(x, axis=0, keepdims=True).astype(I32)
            compact[y] = one_hot(iota((PATCH, 512), 0) == place)

    def fill_e(coded):
        e = iota((512, N), 0)
        lane = iota((512, N), 1)
        x = mm(one_hot((e % 8) // 4 * 64 + e // 8 == lane), coded.astype(BF16))
        for c in range(4):
            k = e % 4 + 12 - 4 * c
            z = jnp.where(lane == k, 16.0 * x, jnp.where(lane == k + CAP, x, 0.0))
            place = jnp.sum(z, axis=1, keepdims=True).astype(I32)
            known = CHUNK * (c + 1)
            e_pick[c, :, 0:known] = one_hot(iota((512, known), 1) == place)

    lane = iota((1, WIDTH), 1) // (WIDTH // HEADS)
    upper = iota((512, N), 0) % 8 < 4

    def score(c, h, s_ref):
        rows = q[c * CHUNK : (c + 1) * CHUNK, :]
        s_ref[...] = mm(jnp.where(lane == h, rows, 0).astype(BF16), kt[...])

    def mix(h, w_ref):
        acc[...] = jnp.where(lane == h, mm(w_ref[...], v[...]), acc[...])

    for b in range(BLOCKS):
        coded = places(b)
        fill_compact(coded)
        fill_e(coded)

        for i in range(4):
            y = lax.rem(my_y + 4 - i, 4)
            size = 31 if i == 0 else 32
            many(fwd.at[b, pl.ds(0, size)], fwd_ss.at[b], fwd_rs.at[b, i]).wait_recv()
            rows = mm(compact[y], fwd[b, pl.ds(y * 32, 32)].reshape(512, WIDTH))
            gathered[...] = rows if i == 0 else gathered[...] + rows
        many(fwd.at[b, pl.ds(0, N - 1)], fwd_ss.at[b], fwd_rs.at[b, 0]).wait_send()
        if b == 0:
            for load in loads:
                load.wait()

        for r in range(0, PATCH, 256):
            rows = gathered[r : r + 256, :].astype(BF16)
            serial[r : r + 256, :] = rows
            normed = layer_norm(rows, gains[b, 0:1, :])
            projected = mm(normed, wqkv[b]).astype(BF16)
            q[r : r + 256, :] = projected[:, 0:WIDTH] * jnp.asarray(0.25, BF16)
            kt[:, r : r + 256] = projected[:, WIDTH : 2 * WIDTH].astype(F32).T.astype(BF16)
            v[r : r + 256, :] = projected[:, 2 * WIDTH :]

        score(0, 0, s0)
        score(0, 1, s1)
        soften(s0, w0)
        for c in range(4):

            def body(j, carry):
                h = 2 * j + 1
                score(c, h + 1, s0)
                soften(s1, w1)
                mix(h - 1, w0)
                score(c, h + 2, s1)
                soften(s0, w0)
                mix(h, w1)
                return carry

            lax.fori_loop(0, HEADS // 2 - 1, body, 0)
            if c < 3:
                score(c + 1, 0, s0)
            soften(s1, w1)
            mix(HEADS - 2, w0)
            if c < 3:
                score(c + 1, 1, s1)
                soften(s0, w0)
            mix(HEADS - 1, w1)

            g = c * CHUNK
            branch = mm(acc[...].astype(BF16), wproj[b])
            middle = (serial[g : g + CHUNK, :].astype(F32) + branch).astype(BF16)
            second = layer_norm(middle, gains[b, 1:2, :])
            up = mm(second, wup[b])
            lifted = (up * (1.0 + lax.erf(up * (0.5**0.5))) * 0.5).astype(BF16)
            finished[g : g + CHUNK, :] = (middle.astype(F32) + mm(lifted, wdown[b])).astype(BF16)

            known = CHUNK * (c + 1)
            rows = mm(e_pick[c, :, 0:known], finished[0:known, :])
            lo, hi = rows[:, 0:N], rows[:, N:]
            first = jnp.where(upper, lo, pltpu.roll(hi, 4, 0)).astype(BF16)
            second = jnp.where(upper, pltpu.roll(lo, 508, 0), hi).astype(BF16)
            ret_send[c, 0:64] = first.reshape(64, 8, N)
            ret_send[c, 64:N] = second.reshape(64, 8, N)

            def give_back(i):
                t = lax.rem(me + i, N)
                remote(
                    ret_send.at[c, t], ret.at[b, c, me], ret_ss.at[b, c], ret_rs.at[b, c], t
                ).start()

            repeat(1, N, 6, give_back)
            ret[b, c, me] = ret_send[c, me]

        for c in range(4):
            d = many(ret.at[b, c, pl.ds(0, N - 1)], ret_ss.at[b, c], ret_rs.at[b, c])
            d.wait_send()
            d.wait_recv()
            z0 = ret[b, c, 0:64].reshape(512, N).astype(F32)
            z1 = ret[b, c, 64:N].reshape(512, N).astype(F32)
            lo = jnp.where(upper, z0, pltpu.roll(z1, 4, 0)).astype(BF16)
            hi = jnp.where(upper, pltpu.roll(z0, 508, 0), z1).astype(BF16)
            part = mm(r_pick[c], jnp.concatenate([lo, hi], axis=1))
            gathered[...] = part if c == 0 else gathered[...] + part
        if b + 1 < BLOCKS:
            current[...] = gathered[...].astype(BF16)
            for i in range(4):
                stage(i, current)
                launch(b + 1, i)
            fill_r(b + 1)
        else:
            out[...] = gathered[...].astype(BF16)


def per_device(points, order, norm_gains, qkv_weight, proj_weight, up_weight, down_weight):
    vm = pl.BlockSpec(memory_space=pltpu.VMEM)
    hbm = pl.BlockSpec(memory_space=pl.ANY)
    dma = pltpu.SemaphoreType.DMA
    return pl.pallas_call(
        kernel,
        out_shape=jax.ShapeDtypeStruct((PATCH, WIDTH), BF16),
        in_specs=[vm] * 3 + [hbm] * 4,
        out_specs=vm,
        scratch_shapes=[
            pltpu.VMEM((BLOCKS, WIDTH, 3 * WIDTH), BF16),
            pltpu.VMEM((BLOCKS, WIDTH, WIDTH), BF16),
            pltpu.VMEM((BLOCKS, WIDTH, MLP), BF16),
            pltpu.VMEM((BLOCKS, MLP, WIDTH), BF16),
            pltpu.VMEM((PATCH, WIDTH), BF16),
            pltpu.VMEM((N, CAP, WIDTH), BF16),
            pltpu.VMEM((BLOCKS, N, CAP, WIDTH), BF16),
            pltpu.VMEM((4, N, 8, N), BF16),
            pltpu.VMEM((BLOCKS, 4, N, 8, N), BF16),
            pltpu.VMEM((8, N), F32),
            pltpu.VMEM((N, 8, N), F32),
            pltpu.VMEM((4, PATCH, 512), BF16),
            pltpu.VMEM((4, 512, PATCH), BF16),
            pltpu.VMEM((4, PATCH, 512), BF16),
            pltpu.VMEM((4, 512, PATCH), BF16),
            pltpu.VMEM((PATCH, WIDTH), F32),
            pltpu.VMEM((PATCH, WIDTH), BF16),
            pltpu.VMEM((PATCH, WIDTH), BF16),
            pltpu.VMEM((WIDTH, PATCH), BF16),
            pltpu.VMEM((PATCH, WIDTH), BF16),
            pltpu.VMEM((CHUNK, WIDTH), F32),
            pltpu.VMEM((CHUNK, PATCH), F32),
            pltpu.VMEM((CHUNK, PATCH), F32),
            pltpu.VMEM((CHUNK, PATCH), BF16),
            pltpu.VMEM((CHUNK, PATCH), BF16),
            pltpu.VMEM((PATCH, WIDTH), BF16),
            dma((BLOCKS,)), dma((BLOCKS, 4)),
            dma((BLOCKS, 4)), dma((BLOCKS, 4)),
            dma, dma, dma((4,)),
        ],
        compiler_params=pltpu.CompilerParams(
            collective_id=0, has_side_effects=True, vmem_limit_bytes=56 * 2**20
        ),
        name="encoder",
    )(points, order, norm_gains, qkv_weight, proj_weight, up_weight, down_weight)


def solution(mesh):
    in_specs = (P(("rep", "pts"), None), P(None, ("rep", "pts")), P(), P(), P(), P(), P())
    out_specs = P(("rep", "pts"), None)
    return jax.shard_map(
        per_device, mesh=mesh, in_specs=in_specs, out_specs=out_specs, check_vma=False
    )
```

```python
import functools

import jax
import jax.numpy as jnp
from jax import lax
from jax.experimental import pallas as pl
from jax.experimental.pallas import tpu as pltpu
from jax.sharding import PartitionSpec as P

HEADS = 16
PATCH = 1024
BLOCKS = 2
WIDTH = 256
MLP = 1024
N = 128
CAP = 16
CHUNK = 256
EPS = 1e-05

F32 = jnp.float32
BF16 = jnp.bfloat16
I32 = jnp.int32
MESH = pl.DeviceIdType.MESH


def iota(shape, dim):
    return lax.broadcasted_iota(I32, shape, dim)


def one_hot(mask):
    return jnp.where(mask, 1.0, 0.0).astype(BF16)


def mm(a, b):
    return jnp.dot(a, b, preferred_element_type=F32)


def mm_nt(a, b):
    return lax.dot_general(a, b, (((1,), (1,)), ((), ())), preferred_element_type=F32)


def layer_norm(features, gain):
    features = features.astype(F32)
    average = jnp.mean(features, axis=-1, keepdims=True)
    centered = features - average
    variance = jnp.mean(centered * centered, axis=-1, keepdims=True)
    return (centered * lax.rsqrt(variance + EPS) * gain).astype(BF16)


def soften(s_ref, w_ref):
    for r in range(0, CHUNK, 16):
        s = s_ref[r : r + 16, :]
        p = jnp.exp(s - jnp.max(s, axis=1, keepdims=True))
        w_ref[r : r + 16, :] = (p * (1.0 / jnp.sum(p, axis=1, keepdims=True))).astype(BF16)


def repeat(low, high, width, body):
    steps = (high - low) // width

    @pl.loop(0, steps)
    def _(j):
        for u in range(width):
            body(low + j * width + u)

    for i in range(low + steps * width, high):
        body(i)


RING = (2, 1, 3, 0)
SQUARE = sorted(
    [(dx, dy) for dx in range(4) for dy in range(4)],
    key=lambda d: -(min(d[0], 4 - d[0]) + min(d[1], 4 - d[1])),
)


def far_first(body, last):
    @pl.loop(0, 7)
    def _(n):
        body(4 + (n + 1) // 2 * (1 - 2 * lax.rem(n, 2)))

    last(0)


def kernel(
    points, order, gains, wqkv_hbm, wproj_hbm, wup_hbm, wdown_hbm,
    out,
    wqkv, wproj, wup, wdown,
    current, send, fwd, ret_send, ret, counts_send, counts,
    compact, g_pick, r_pick, e_pick,
    gathered, serial, q, kt, v, acc, s0, s1, w0, w1, finished,
    fwd_ss, fwd_rs, ret_ss, ret_rs, cnt_ss, cnt_rs, load_sem,
):
    me = lax.axis_index("pts")
    my_y = lax.rem(me, 4)
    my_j = me // 4
    my_x = lax.rem(my_j, 4)
    my_z = me // 16
    barrier = pltpu.get_barrier_semaphore()

    repeat(
        1, N, 6,
        lambda i: pl.semaphore_signal(
            barrier, inc=1, device_id={"pts": lax.rem(me + i, N)}, device_id_type=MESH
        ),
    )
    loads = [
        pltpu.make_async_copy(a, b, load_sem.at[i])
        for i, (a, b) in enumerate(
            ((wqkv_hbm, wqkv), (wproj_hbm, wproj), (wup_hbm, wup), (wdown_hbm, wdown))
        )
    ]
    for load in loads:
        load.start()

    def remote(src, dst, ss, rs, t):
        return pltpu.make_async_remote_copy(
            src_ref=src, dst_ref=dst, send_sem=ss, recv_sem=rs,
            device_id={"pts": t}, device_id_type=MESH,
        )

    def many(part, ss, rs):
        return remote(part, part, ss, rs, lax.rem(me + 1, N))

    def plan(b):
        target = order[pl.ds(b, 1), :] // PATCH
        to = one_hot(iota((N, PATCH), 0) == target)
        before = one_hot(iota((PATCH, PATCH), 0) < iota((PATCH, PATCH), 1))
        rank = jnp.sum(to.astype(F32) * mm(to, before), axis=0, keepdims=True).astype(I32)
        count = mm_nt(jnp.ones((8, PATCH), BF16), to)
        return target, rank, count

    plans = [plan(b) for b in range(BLOCKS)]
    counts_send[...] = plans[0][2] + 32.0 * plans[1][2]

    def fill_g(b):
        target, rank, _ = plans[b]
        slot = (target // 4) * CAP + rank
        for y in range(4):
            mine = jnp.where(lax.rem(target, 4) == y, slot, -1)
            g_pick[y] = one_hot(iota((32 * CAP, PATCH), 0) == mine)

    def fill_r(b):
        target = jnp.broadcast_to(plans[b][0].astype(F32), (N, PATCH)).T.astype(I32)[:, 0:1]
        rank = jnp.broadcast_to(plans[b][1].astype(F32), (N, PATCH)).T.astype(I32)[:, 0:1]
        place = (target % 64) * 8 + (target // 64) * 4
        for c in range(4):
            low = 12 - 4 * c
            here = (rank >= low) & (rank < low + 4)
            slot = jnp.where(here, place + rank - low, -1)
            r_pick[c] = one_hot(iota((PATCH, 512), 1) == slot)

    def stage(i, rows_ref):
        y = lax.rem(my_y + i, 4)
        rows = mm(g_pick[y], rows_ref[...]).astype(BF16).reshape(32, CAP, WIDTH)
        send[pl.ds(y * 32, 32)] = rows

    def launch(b, i):
        y = lax.rem(my_y + i, 4)

        def one(dz, dx):
            tj = lax.rem(my_z + dz, 8) * 4 + lax.rem(my_x + dx, 4)
            remote(
                send.at[y * 32 + tj], fwd.at[b, my_y * 32 + my_j],
                fwd_ss.at[b], fwd_rs.at[b, i], tj * 4 + y,
            ).start()

        def row(dz):
            for dx in RING:
                one(dz, dx)

        def own_row(dz):
            for dx in RING[:3]:
                one(dz, dx)

        if i == 0:
            fwd[b, my_y * 32 + my_j] = send[my_y * 32 + my_j]
        far_first(row, own_row if i == 0 else row)

    fill_g(0)
    for i in RING:
        stage(i, points)

    pl.semaphore_wait(barrier, N - 1)

    repeat(
        1, N, 6,
        lambda i: remote(
            counts_send.at[pl.ds(0, 1), :], counts.at[me, pl.ds(0, 1), :], cnt_ss, cnt_rs,
            lax.rem(me + i, N),
        ).start(),
    )
    counts[me] = counts_send[...]
    for i in RING:
        launch(0, i)

    fill_g(1)
    fill_r(0)

    d = many(counts.at[pl.ds(0, N - 1), pl.ds(0, 1), :], cnt_ss, cnt_rs)
    d.wait_send()
    d.wait_recv()
    table = counts[:, 0, :].astype(I32)

    def places(b):
        count = (table % 32) if b == 0 else (table // 32)
        mine = one_hot(iota((N, N), 0) == me)
        n = mm(count.astype(F32).astype(BF16), mine)
        lane = iota((N, N), 1)
        slot = lane % CAP
        valid = n > slot.astype(F32)
        used = one_hot(valid)
        above = one_hot(iota((N, N), 0) > iota((N, N), 1))
        earlier = mm(above, used)
        total = mm(jnp.ones((N, N), BF16), used).astype(BF16)
        higher = one_hot((iota((N, N), 0) > slot) & (iota((N, N), 0) < CAP))
        place = jnp.where(valid, (earlier + mm(total, higher)).astype(I32), -1)
        coded = jnp.where(lane < CAP, place >> 4, jnp.where(lane < 2 * CAP, place & 15, 0))
        return coded.astype(F32)

    def fill_compact(coded):
        coded_t = coded.T.astype(BF16)[0 : 2 * CAP, :]
        row = iota((2 * CAP, 512), 0)
        k = iota((2 * CAP, 512), 1) % CAP
        for y in range(4):
            x = mm(coded_t, one_hot(iota((N, 512), 0) == iota((N, 512), 1) // CAP * 4 + y))
            x = jnp.where(row == k, 16.0 * x, jnp.where(row == k + CAP, x, 0.0))
            place = jnp.sum(x, axis=0, keepdims=True).astype(I32)
            compact[y] = one_hot(iota((PATCH, 512), 0) == place)

    def fill_e(coded):
        e = iota((512, N), 0)
        lane = iota((512, N), 1)
        x = mm(one_hot((e % 8) // 4 * 64 + e // 8 == lane), coded.astype(BF16))
        for c in range(4):
            k = e % 4 + 12 - 4 * c
            z = jnp.where(lane == k, 16.0 * x, jnp.where(lane == k + CAP, x, 0.0))
            place = jnp.sum(z, axis=1, keepdims=True).astype(I32)
            known = CHUNK * (c + 1)
            e_pick[c, :, 0:known] = one_hot(iota((512, known), 1) == place)

    lane = iota((1, WIDTH), 1) // (WIDTH // HEADS)
    upper = iota((512, N), 0) % 8 < 4

    def score(c, h, s_ref):
        rows = q[c * CHUNK : (c + 1) * CHUNK, :]
        s_ref[...] = mm(jnp.where(lane == h, rows, 0).astype(BF16), kt[...])

    def mix(h, w_ref):
        acc[...] = jnp.where(lane == h, mm(w_ref[...], v[...]), acc[...])

    for b in range(BLOCKS):
        coded = places(b)
        fill_compact(coded)
        fill_e(coded)

        for i in RING:
            y = lax.rem(my_y + 4 - i, 4)
            size = 31 if i == 0 else 32
            many(fwd.at[b, pl.ds(0, size)], fwd_ss.at[b], fwd_rs.at[b, i]).wait_recv()
            rows = mm(compact[y], fwd[b, pl.ds(y * 32, 32)].reshape(512, WIDTH))
            gathered[...] = rows if i == RING[0] else gathered[...] + rows
        many(fwd.at[b, pl.ds(0, N - 1)], fwd_ss.at[b], fwd_rs.at[b, 0]).wait_send()
        if b == 0:
            for load in loads:
                load.wait()

        for r in range(0, PATCH, 256):
            rows = gathered[r : r + 256, :].astype(BF16)
            serial[r : r + 256, :] = rows
            normed = layer_norm(rows, gains[b, 0:1, :])
            projected = mm(normed, wqkv[b]).astype(BF16)
            q[r : r + 256, :] = projected[:, 0:WIDTH] * jnp.asarray(0.25, BF16)
            kt[:, r : r + 256] = projected[:, WIDTH : 2 * WIDTH].astype(F32).T.astype(BF16)
            v[r : r + 256, :] = projected[:, 2 * WIDTH :]

        score(0, 0, s0)
        score(0, 1, s1)
        soften(s0, w0)
        for c in range(4):

            def body(j, carry):
                h = 2 * j + 1
                score(c, h + 1, s0)
                soften(s1, w1)
                mix(h - 1, w0)
                score(c, h + 2, s1)
                soften(s0, w0)
                mix(h, w1)
                return carry

            lax.fori_loop(0, HEADS // 2 - 1, body, 0)
            if c < 3:
                score(c + 1, 0, s0)
            soften(s1, w1)
            mix(HEADS - 2, w0)
            if c < 3:
                score(c + 1, 1, s1)
                soften(s0, w0)
            mix(HEADS - 1, w1)

            g = c * CHUNK
            branch = mm(acc[...].astype(BF16), wproj[b])
            middle = (serial[g : g + CHUNK, :].astype(F32) + branch).astype(BF16)
            second = layer_norm(middle, gains[b, 1:2, :])
            up = mm(second, wup[b])
            lifted = (up * (1.0 + lax.erf(up * (0.5**0.5))) * 0.5).astype(BF16)
            finished[g : g + CHUNK, :] = (middle.astype(F32) + mm(lifted, wdown[b])).astype(BF16)

            known = CHUNK * (c + 1)
            rows = mm(e_pick[c, :, 0:known], finished[0:known, :])
            lo, hi = rows[:, 0:N], rows[:, N:]
            first = jnp.where(upper, lo, pltpu.roll(hi, 4, 0)).astype(BF16)
            second = jnp.where(upper, pltpu.roll(lo, 508, 0), hi).astype(BF16)
            ret_send[c, 0:64] = first.reshape(64, 8, N)
            ret_send[c, 64:N] = second.reshape(64, 8, N)

            def give_back(dz, square):
                for dx, dy in square:
                    t = lax.rem(my_z + dz, 8) * 16 + lax.rem(my_x + dx, 4) * 4
                    t = t + lax.rem(my_y + dy, 4)
                    remote(
                        ret_send.at[c, t], ret.at[b, c, me], ret_ss.at[b, c], ret_rs.at[b, c], t
                    ).start()

            far_first(lambda dz: give_back(dz, SQUARE), lambda dz: give_back(dz, SQUARE[:-1]))
            ret[b, c, me] = ret_send[c, me]

        for c in range(4):
            d = many(ret.at[b, c, pl.ds(0, N - 1)], ret_ss.at[b, c], ret_rs.at[b, c])
            d.wait_send()
            d.wait_recv()
            z0 = ret[b, c, 0:64].reshape(512, N).astype(F32)
            z1 = ret[b, c, 64:N].reshape(512, N).astype(F32)
            lo = jnp.where(upper, z0, pltpu.roll(z1, 4, 0)).astype(BF16)
            hi = jnp.where(upper, pltpu.roll(z0, 508, 0), z1).astype(BF16)
            part = mm(r_pick[c], jnp.concatenate([lo, hi], axis=1))
            gathered[...] = part if c == 0 else gathered[...] + part
        if b + 1 < BLOCKS:
            current[...] = gathered[...].astype(BF16)
            for i in RING:
                stage(i, current)
                launch(b + 1, i)
            fill_r(b + 1)
        else:
            out[...] = gathered[...].astype(BF16)


def per_device(points, order, norm_gains, qkv_weight, proj_weight, up_weight, down_weight):
    vm = pl.BlockSpec(memory_space=pltpu.VMEM)
    hbm = pl.BlockSpec(memory_space=pl.ANY)
    dma = pltpu.SemaphoreType.DMA
    return pl.pallas_call(
        kernel,
        out_shape=jax.ShapeDtypeStruct((PATCH, WIDTH), BF16),
        in_specs=[vm] * 3 + [hbm] * 4,
        out_specs=vm,
        scratch_shapes=[
            pltpu.VMEM((BLOCKS, WIDTH, 3 * WIDTH), BF16),
            pltpu.VMEM((BLOCKS, WIDTH, WIDTH), BF16),
            pltpu.VMEM((BLOCKS, WIDTH, MLP), BF16),
            pltpu.VMEM((BLOCKS, MLP, WIDTH), BF16),
            pltpu.VMEM((PATCH, WIDTH), BF16),
            pltpu.VMEM((N, CAP, WIDTH), BF16),
            pltpu.VMEM((BLOCKS, N, CAP, WIDTH), BF16),
            pltpu.VMEM((4, N, 8, N), BF16),
            pltpu.VMEM((BLOCKS, 4, N, 8, N), BF16),
            pltpu.VMEM((8, N), F32),
            pltpu.VMEM((N, 8, N), F32),
            pltpu.VMEM((4, PATCH, 512), BF16),
            pltpu.VMEM((4, 512, PATCH), BF16),
            pltpu.VMEM((4, PATCH, 512), BF16),
            pltpu.VMEM((4, 512, PATCH), BF16),
            pltpu.VMEM((PATCH, WIDTH), F32),
            pltpu.VMEM((PATCH, WIDTH), BF16),
            pltpu.VMEM((PATCH, WIDTH), BF16),
            pltpu.VMEM((WIDTH, PATCH), BF16),
            pltpu.VMEM((PATCH, WIDTH), BF16),
            pltpu.VMEM((CHUNK, WIDTH), F32),
            pltpu.VMEM((CHUNK, PATCH), F32),
            pltpu.VMEM((CHUNK, PATCH), F32),
            pltpu.VMEM((CHUNK, PATCH), BF16),
            pltpu.VMEM((CHUNK, PATCH), BF16),
            pltpu.VMEM((PATCH, WIDTH), BF16),
            dma((BLOCKS,)), dma((BLOCKS, 4)),
            dma((BLOCKS, 4)), dma((BLOCKS, 4)),
            dma, dma, dma((4,)),
        ],
        compiler_params=pltpu.CompilerParams(
            collective_id=0, has_side_effects=True, vmem_limit_bytes=56 * 2**20
        ),
        name="encoder",
    )(points, order, norm_gains, qkv_weight, proj_weight, up_weight, down_weight)


def solution(mesh):
    in_specs = (P(("rep", "pts"), None), P(None, ("rep", "pts")), P(), P(), P(), P(), P())
    out_specs = P(("rep", "pts"), None)
    return jax.shard_map(
        per_device, mesh=mesh, in_specs=in_specs, out_specs=out_specs, check_vma=False
    )
```
